32 devices in a mesh: groups: 2 (over y), mesh: 8 (over z, x), sub: 2 (over core).
Axes of the slice: x: 2, y: 2, z: 4, core: 2. Of those that a mesh axis runs over, the one named last changes fastest.
Arguments:
- inputs: bfloat16 [65536, 227], P(('groups', 'mesh', 'sub')), parts along dimension 0, may hold values from -6 to 6
- targets: bfloat16 [65536, 227], P(('groups', 'mesh', 'sub')), parts along dimension 0, may hold values from -6 to 6
- node_weight: float32 [32768], P(('mesh', 'sub')), may hold values from 0.3 to 8, as said below
- w_embed: bfloat16 [227, 512], replicated, may hold values from -0.375 to 0.375
- w_mix: bfloat16 [512, 512], replicated, may hold values from -0.25 to 0.25
- w_back: bfloat16 [512, 512], replicated, may hold values from -0.25 to 0.25
- head_projection_weight: bfloat16 [512, 227], replicated, may hold values from -0.25 to 0.25
- enc_src: int32 [16, 5, 1024], P(('mesh', 'sub')), may hold values from 0 to 2047
- enc_dst: int32 [16, 5, 1024], P(('mesh', 'sub')), may hold values from 0 to 319
- enc_weight: float32 [16, 5, 1024], P(('mesh', 'sub')), may hold values from 0.25 to 1
- enc_count: int32 [16, 5], P(('mesh', 'sub')), may hold values from 256 to 1024, as said below
- proc_src: int32 [16, 2176], P(('mesh', 'sub')), may hold values from 0 to 5119, as said below
- proc_dst: int32 [16, 2176], P(('mesh', 'sub')), may hold values from 0 to 319
- proc_weight: float32 [16, 2176], P(('mesh', 'sub')), may hold values from 0.25 to 1
- proc_count: int32 [16], P(('mesh', 'sub')), may hold values from 1088 to 2176, as said below
- far_src: int32 [256, 4], P(('mesh', 'sub')), may hold values from 0 to 319
- far_dst: int32 [256, 4], P(('mesh', 'sub')), may hold values from 0 to 319
- far_weight: float32 [256, 4], P(('mesh', 'sub')), may hold values from -8 to 8
- far_count: int32 [256], P(('mesh', 'sub')), may hold values from 1 to 4, as said below
- dec_src: int32 [16, 5, 2048], P(('mesh', 'sub')), may hold values from 0 to 319
- dec_dst: int32 [16, 5, 2048], P(('mesh', 'sub')), may hold values from 0 to 2047
- dec_weight: float32 [16, 5, 2048], P(('mesh', 'sub')), may hold values from 0.25 to 1
- dec_count: int32 [16, 5], P(('mesh', 'sub')), may hold values from 512 to 2048, as said below
Outputs:
- prediction: bfloat16 [65536, 227], P(('groups', 'mesh', 'sub')), parts along dimension 0
- input_gradient: bfloat16 [65536, 227], P(('groups', 'mesh', 'sub')), parts along dimension 0
- embedding_weight_gradient: float32 [454, 512], P('groups'), parts along dimension 0
- mixing_weight_gradient: float32 [1024, 512], P('groups'), parts along dimension 0
- backward_weight_gradient: float32 [1024, 512], P('groups'), parts along dimension 0
- head_weight_gradient: float32 [1024, 227], P('groups'), parts along dimension 0
- loss: float32 [2], P('groups'), parts along dimension 0
The draws below stay inside these ranges and needn't reach their ends.
There are 2 independent parts, one for each index of `groups`. The reference program is written for one: setup_inputs(seed, part) draws one part's arguments, and reference() takes and returns one part's arrays. A program takes and returns all parts, laid end to end along the dimension named above; an argument that names none is the same for every part. Nothing has to cross between parts.
Inputs may be any that keep to these rules, and one draw needn't show every extreme that they name: `enc_count`: in every draw all blocks whose partner is some one mesh shard have all 1024 slots live. `dec_count`: in every draw all blocks whose partner is some one mesh shard have all 2048 slots live. `proc_count`: some shard has all 2176 slots live in every draw. `proc_src`: row q holds mesh nodes q * 320 - 32 to (q + 1) * 320 + 31, taken modulo 5120. `far_count`: in every draw some destination shard has all 4 slots live from every owner. `node_weight`: positive weights.
All inputs are finite; a program needn't handle non-finite values.
Results may differ from the reference program's by a relative error of at most 0.013.
Values may be sent and summed in bfloat16 or wider, within the bound.
A program may use at most 192 MiB of HBM per device.

```python
import jax
import jax.numpy as jnp
from jax import lax

C = 227
L = 512
G_DEV = 2048
M_DEV = 320
REACH = 2
EDGES_P = 2176
CAP_F = 4
HALO = 32
CAP_E = 1024
CAP_D = 2048
SHARDS = 16
GRID = 32768
MESH = 5120


def near_counts(key, capacity):
    first_key, second_key = jax.random.split(key)
    span = 2 * REACH + 1
    counts = jax.random.randint(first_key, (SHARDS, span), capacity // 4, capacity + 1)
    busiest = jax.random.randint(second_key, (), 0, SHARDS)
    partner = jnp.mod(jnp.arange(SHARDS)[:, None] + jnp.arange(span)[None, :] - REACH, SHARDS)
    return jnp.where(partner == busiest, capacity, counts).astype(jnp.int32)


def draw_enc_count(key, part):
    key = jax.random.fold_in(key, 11)
    return near_counts(key, CAP_E)


def draw_dec_count(key, part):
    key = jax.random.fold_in(key, 12)
    return near_counts(key, CAP_D)


def draw_proc_count(key, part):
    key = jax.random.fold_in(key, 13)
    first_key, second_key = jax.random.split(key)
    counts = jax.random.randint(first_key, (SHARDS,), EDGES_P // 2, EDGES_P + 1)
    busiest = jax.random.randint(second_key, (), 0, SHARDS)
    return jnp.where(jnp.arange(SHARDS) == busiest, EDGES_P, counts).astype(jnp.int32)


def draw_proc_src(key, part):
    key = jax.random.fold_in(key, 14)
    inner_key, rim_key, pick_key = jax.random.split(key, 3)
    inner = jax.random.randint(inner_key, (SHARDS, EDGES_P), 0, M_DEV)
    rim_pick = jax.random.randint(rim_key, (SHARDS, EDGES_P), 0, 2 * HALO)
    rim_offset = jnp.where(rim_pick < HALO, rim_pick - HALO, M_DEV + rim_pick - HALO)
    choose_rim = jax.random.randint(pick_key, (SHARDS, EDGES_P), 0, 2) == 0
    offset = jnp.where(choose_rim, rim_offset, inner)
    base = jnp.arange(SHARDS, dtype=jnp.int32)[:, None] * M_DEV
    return jnp.mod(base + offset, M_DEV * SHARDS).astype(jnp.int32)


def draw_far_count(key, part):
    key = jax.random.fold_in(key, 16)
    first_key, second_key = jax.random.split(key)
    counts = jax.random.randint(first_key, (SHARDS, SHARDS), 1, CAP_F + 1)
    busiest = jax.random.randint(second_key, (), 0, SHARDS)
    row = jnp.arange(SHARDS)[:, None] == busiest
    return jnp.where(row, CAP_F, counts).reshape(SHARDS * SHARDS).astype(jnp.int32)


def signed_magnitudes(key, lowest, highest):
    size_key, sign_key = jax.random.split(key)
    shape = (SHARDS * SHARDS, CAP_F)
    exponent = jax.random.uniform(size_key, shape, jnp.float32, jnp.log(lowest), jnp.log(highest))
    sign = jnp.where(jax.random.uniform(sign_key, shape, jnp.float32) < 0.5, -1.0, 1.0)
    return sign * jnp.exp(exponent)


def draw_far_weight(key, part):
    key = jax.random.fold_in(key, 17)
    values = signed_magnitudes(key, 0.5, 4.0)
    return values.astype(jnp.float32)


def draw_node_weight(key, part):
    key = jax.random.fold_in(key, 15)
    position = jnp.arange(GRID).astype(jnp.float32) / max(GRID - 1, 1)
    ramp = 1.0 + 3.0 * position
    factor = jax.random.uniform(key, (GRID,), jnp.float32, 0.5, 1.5)
    return (ramp * factor).astype(jnp.float32)


def plant(values, rng, low, high):
    extent = values.shape
    place = [jax.random.randint(jax.random.fold_in(rng, axis), (), 0, extent[axis]) for axis in range(len(extent))]
    values = values.at[tuple(place)].set(low)
    longest = extent.index(max(extent))
    place[longest] = (place[longest] + 1) % extent[longest]
    return values.at[tuple(place)].set(high)


def block_scale(stream_key, shape, cuts, low, top_value):
    loudness = 1.0
    for axis_at, parts in cuts:
        steps = jax.random.uniform(jax.random.fold_in(jax.random.fold_in(stream_key, 6), axis_at), (parts,), jnp.float32, low / len(cuts), top_value / len(cuts))
        loudness = loudness * jnp.repeat(jnp.exp(steps), shape[axis_at] // parts).reshape((-1,) + (1,) * (len(shape) - 1 - axis_at))
    return loudness


def bell_draw(rng, dims, scale, limit, cuts=(), kind=jnp.bfloat16):
    entries = jax.random.normal(rng, dims, jnp.float32) * scale
    if len(cuts) > 0:
        entries = block_scale(rng, dims, cuts, -0.22, 0.18) * entries
    return jnp.clip(entries, min=-limit, max=limit).astype(kind)


def setup_inputs(seed: int = 0, part: int = 0) -> dict:
    keys = jax.random.split(jax.random.key(seed), 24)
    part_keys = jax.random.split(jax.random.fold_in(keys[23], part), 24)
    return {
        "inputs": bell_draw(part_keys[0], (GRID, C), 1.0, 6.0, ((0, 16),)),
        "targets": bell_draw(part_keys[1], (GRID, C), 1.0, 6.0, ((0, 16),)),
        "node_weight": draw_node_weight(jax.random.fold_in(keys[23], 71), part),
        "w_embed": bell_draw(keys[3], (C, L), C ** -0.5, 0.375),
        "w_mix": bell_draw(keys[4], (L, L), L ** -0.5, 0.25),
        "w_back": bell_draw(keys[5], (L, L), L ** -0.5, 0.25),
        "head_projection_weight": bell_draw(keys[6], (L, C), L ** -0.5, 0.25),
        "enc_src": plant(jax.random.randint(keys[7], (SHARDS, 2 * REACH + 1, CAP_E), 0, G_DEV), jax.random.fold_in(keys[7], 1), 0, G_DEV - 1).astype(jnp.int32),
        "enc_dst": plant(jax.random.randint(keys[8], (SHARDS, 2 * REACH + 1, CAP_E), 0, M_DEV), jax.random.fold_in(keys[8], 1), 0, M_DEV - 1).astype(jnp.int32),
        "enc_weight": jnp.clip(0.25 + 0.75 * jax.random.uniform(keys[9], (SHARDS, 2 * REACH + 1, CAP_E), jnp.float32) ** block_scale(keys[9], (SHARDS, 2 * REACH + 1, CAP_E), ((0, 16),), -0.2, 0.2), 0.25, 1.0),
        "enc_count": draw_enc_count(jax.random.fold_in(keys[23], 71), part),
        "proc_src": draw_proc_src(jax.random.fold_in(keys[23], 71), part),
        "proc_dst": plant(jax.random.randint(keys[12], (SHARDS, EDGES_P), 0, M_DEV), jax.random.fold_in(keys[12], 1), 0, M_DEV - 1).astype(jnp.int32),
        "proc_weight": jnp.clip(0.25 + 0.75 * jax.random.uniform(keys[13], (SHARDS, EDGES_P), jnp.float32) ** block_scale(keys[13], (SHARDS, EDGES_P), ((0, 16),), -0.2, 0.2), 0.25, 1.0),
        "proc_count": draw_proc_count(jax.random.fold_in(keys[23], 71), part),
        "far_src": plant(jax.random.randint(keys[15], (SHARDS * SHARDS, CAP_F), 0, M_DEV), jax.random.fold_in(keys[15], 1), 0, M_DEV - 1).astype(jnp.int32),
        "far_dst": plant(jax.random.randint(keys[16], (SHARDS * SHARDS, CAP_F), 0, M_DEV), jax.random.fold_in(keys[16], 1), 0, M_DEV - 1).astype(jnp.int32),
        "far_weight": draw_far_weight(jax.random.fold_in(keys[23], 71), part),
        "far_count": draw_far_count(jax.random.fold_in(keys[23], 71), part),
        "dec_src": plant(jax.random.randint(keys[19], (SHARDS, 2 * REACH + 1, CAP_D), 0, M_DEV), jax.random.fold_in(keys[19], 1), 0, M_DEV - 1).astype(jnp.int32),
        "dec_dst": plant(jax.random.randint(keys[20], (SHARDS, 2 * REACH + 1, CAP_D), 0, G_DEV), jax.random.fold_in(keys[20], 1), 0, G_DEV - 1).astype(jnp.int32),
        "dec_weight": jnp.clip(0.25 + 0.75 * jax.random.uniform(keys[21], (SHARDS, 2 * REACH + 1, CAP_D), jnp.float32) ** block_scale(keys[21], (SHARDS, 2 * REACH + 1, CAP_D), ((0, 16),), -0.2, 0.2), 0.25, 1.0),
        "dec_count": draw_dec_count(jax.random.fold_in(keys[23], 71), part),
    }


EPS = 1e-05

def norm_scale(values):
    return lax.rsqrt(lax.optimization_barrier(jnp.mean(values * values, axis=-1, keepdims=True)) + EPS)

def norm_back(upstream, normed_f, scale):
    return scale * (upstream - normed_f * lax.optimization_barrier(jnp.mean(upstream * normed_f, axis=-1, keepdims=True)))

def silu_slope(values):
    sigma = jax.nn.sigmoid(values)
    return sigma * (1.0 + values * (1.0 - sigma))

def block_factor(weight, count, column, capacity):
    live_slot = jnp.arange(capacity, dtype=jnp.int32)[None, :] < count[:, column][:, None]
    return jnp.where(live_slot, weight[:, column, :], 0.0).reshape(-1)

def reference(inputs, targets, node_weight, w_embed, w_mix, w_back, head_projection_weight, enc_src, enc_dst, enc_weight, enc_count, proc_src, proc_dst, proc_weight, proc_count, far_src, far_dst, far_weight, far_count, dec_src, dec_dst, dec_weight, dec_count):
    shard_ids = jnp.arange(SHARDS, dtype=jnp.int32)[:, None]
    columns = list(range(2 * REACH + 1))
    partners = [jnp.mod(shard_ids + (column - REACH), SHARDS).astype(jnp.int32) for column in columns]
    pre_embed = jnp.dot(inputs, w_embed, preferred_element_type=jnp.float32)
    embedded = jax.nn.silu(pre_embed).astype(jnp.bfloat16)
    enc_tables = []
    gathered = jnp.zeros((MESH, L), jnp.float32)
    for column in columns:
        factor = block_factor(enc_weight, enc_count, column, CAP_E)
        anchor = (shard_ids * G_DEV + enc_src[:, column, :]).reshape(-1).astype(jnp.int32)
        landing = (partners[column] * M_DEV + enc_dst[:, column, :]).reshape(-1).astype(jnp.int32)
        enc_tables.append((factor, anchor, landing))
        message = (factor[:, None] * embedded[anchor].astype(jnp.float32)).astype(jnp.bfloat16)
        partial_value = jax.ops.segment_sum(message.astype(jnp.float32), landing, num_segments=MESH).astype(jnp.bfloat16)
        gathered = gathered + partial_value.astype(jnp.float32)
    mesh_scale = norm_scale(gathered)
    latent_f = gathered * mesh_scale
    mesh_latent = latent_f.astype(jnp.bfloat16)
    proc_from = proc_src.reshape(-1).astype(jnp.int32)
    proc_to = (shard_ids * M_DEV + proc_dst).reshape(-1).astype(jnp.int32)
    proc_live = jnp.arange(EDGES_P, dtype=jnp.int32)[None, :] < proc_count[:, None]
    proc_factor = jnp.where(proc_live, proc_weight, 0.0).reshape(-1)
    far_local = jnp.transpose(far_src.reshape(SHARDS, SHARDS, CAP_F), (1, 0, 2))
    owner = jnp.arange(SHARDS, dtype=jnp.int32)[None, :, None]
    requester = jnp.arange(SHARDS, dtype=jnp.int32)[:, None, None]
    far_from = (owner * M_DEV + far_local).reshape(-1).astype(jnp.int32)
    far_to = (requester * M_DEV + far_dst.reshape(SHARDS, SHARDS, CAP_F)).reshape(-1).astype(jnp.int32)
    far_live = jnp.arange(CAP_F, dtype=jnp.int32)[None, None, :] < far_count.reshape(SHARDS, SHARDS)[:, :, None]
    far_factor = jnp.where(far_live, far_weight.reshape(SHARDS, SHARDS, CAP_F), 0.0).reshape(-1)
    proc_sum = jax.ops.segment_sum(proc_factor[:, None] * mesh_latent[proc_from].astype(jnp.float32), proc_to, num_segments=MESH)
    proc_sum = proc_sum + jax.ops.segment_sum(far_factor[:, None] * mesh_latent[far_from].astype(jnp.float32), far_to, num_segments=MESH)
    mixed_in = mesh_latent.astype(jnp.float32) + proc_sum
    proc_scale = norm_scale(mixed_in)
    proc_norm = mixed_in * proc_scale
    normed = proc_norm.astype(jnp.bfloat16)
    pre_mix = jnp.dot(normed, w_mix, preferred_element_type=jnp.float32)
    hidden = jax.nn.silu(pre_mix).astype(jnp.bfloat16)
    processed = (mesh_latent.astype(jnp.float32) + jnp.dot(hidden, w_back, preferred_element_type=jnp.float32)).astype(jnp.bfloat16)
    dec_tables = []
    decoded = jnp.zeros((GRID, L), jnp.float32)
    for column in columns:
        factor = block_factor(dec_weight, dec_count, column, CAP_D)
        anchor = (partners[column] * M_DEV + dec_src[:, column, :]).reshape(-1).astype(jnp.int32)
        landing = (shard_ids * G_DEV + dec_dst[:, column, :]).reshape(-1).astype(jnp.int32)
        dec_tables.append((factor, anchor, landing))
        message = (factor[:, None] * processed[anchor].astype(jnp.float32)).astype(jnp.bfloat16)
        decoded = decoded + jax.ops.segment_sum(message.astype(jnp.float32), landing, num_segments=GRID)
    grid_in = embedded.astype(jnp.float32) + decoded
    grid_scale = norm_scale(grid_in)
    grid_norm = grid_in * grid_scale
    grid_node_state = grid_norm.astype(jnp.bfloat16)
    predicted_fields = jnp.dot(grid_node_state, head_projection_weight, preferred_element_type=jnp.float32)
    residual_error = predicted_fields - targets.astype(jnp.float32)
    loss = (0.5 * jnp.sum(node_weight[:, None] * residual_error * residual_error) / GRID).reshape(1)
    weighted_error = (node_weight[:, None] * residual_error).astype(jnp.bfloat16)
    d_state = jnp.dot(weighted_error, head_projection_weight.T, preferred_element_type=jnp.float32)
    d_grid = norm_back(d_state, grid_norm, grid_scale)
    d_processed = jnp.zeros((MESH, L), jnp.float32)
    for column in columns:
        factor, anchor, landing = dec_tables[column]
        term = (factor[:, None] * d_grid[landing]).astype(jnp.bfloat16)
        partial_value = jax.ops.segment_sum(term.astype(jnp.float32), anchor, num_segments=MESH).astype(jnp.bfloat16)
        d_processed = d_processed + partial_value.astype(jnp.float32)
    processed_grad = d_processed.astype(jnp.bfloat16)
    d_pre_mix = (jnp.dot(processed_grad, w_back.T, preferred_element_type=jnp.float32) * silu_slope(pre_mix)).astype(jnp.bfloat16)
    d_normed = jnp.dot(d_pre_mix, w_mix.T, preferred_element_type=jnp.float32)
    d_proc = norm_back(d_normed, proc_norm, proc_scale)
    spread = jax.ops.segment_sum(proc_factor[:, None] * d_proc[proc_to], proc_from, num_segments=MESH)
    far_term = (far_factor[:, None] * d_proc[far_to]).astype(jnp.bfloat16)
    spread = spread + jax.ops.segment_sum(far_term.astype(jnp.float32), far_from, num_segments=MESH)
    d_latent = d_processed + d_proc + spread
    d_gathered = norm_back(d_latent, latent_f, mesh_scale)
    enc_back = d_gathered.astype(jnp.bfloat16)
    d_embedded = d_grid
    for column in columns:
        factor, anchor, landing = enc_tables[column]
        d_embedded = d_embedded + jax.ops.segment_sum(factor[:, None] * enc_back[landing].astype(jnp.float32), anchor, num_segments=GRID)
    d_pre_embed = (d_embedded * silu_slope(pre_embed)).astype(jnp.bfloat16)
    input_gradient = jnp.dot(d_pre_embed, w_embed.T, preferred_element_type=jnp.float32).astype(jnp.bfloat16)
    embedding_weight_gradient = jnp.dot(inputs.T, d_pre_embed, preferred_element_type=jnp.float32) / GRID
    mixing_weight_gradient = jnp.dot(normed.T, d_pre_mix, preferred_element_type=jnp.float32) / GRID
    backward_weight_gradient = jnp.dot(hidden.T, processed_grad, preferred_element_type=jnp.float32) / GRID
    head_weight_gradient = jnp.dot(grid_node_state.T, weighted_error, preferred_element_type=jnp.float32) / GRID
    return (predicted_fields.astype(jnp.bfloat16), input_gradient, embedding_weight_gradient, mixing_weight_gradient, backward_weight_gradient, head_weight_gradient, loss)
```

```python
import jax
import jax.numpy as jnp
from jax import lax
from jax.sharding import PartitionSpec as P

M_DEV = 320
REACH = 2
HALO = 32


EPS = 1e-05


def passed_along(block, axis, distance):
    devices = range(lax.axis_size(axis))
    route = [((i - distance) % len(devices), i) for i in devices]
    return lax.ppermute(block, axis, route)


def norm_scale(values):
    return lax.rsqrt(jnp.mean(values * values, axis=-1, keepdims=True) + EPS)


def norm_back(upstream, normed_f, scale):
    return scale * (upstream - normed_f * jnp.mean(upstream * normed_f, axis=-1, keepdims=True))


def silu_slope(values):
    sigma = jax.nn.sigmoid(values)
    return sigma * (1.0 + values * (1.0 - sigma))


def slot_factor(weight, count):
    live_slot = lax.broadcasted_iota(jnp.int32, weight.shape, 1) < count[:, None]
    return jnp.where(live_slot, weight, 0.0)


def one_hot(index, total, factor=None):
    rows = lax.broadcasted_iota(jnp.int32, index.shape[:-1] + (total, index.shape[-1]), index.ndim - 1)
    hit = rows == index[..., None, :]
    marks = 1.0 if factor is None else factor[..., None, :]
    return jnp.where(hit, marks, 0.0).astype(jnp.bfloat16)


def edge_matrix(factor, to, to_total, start, start_total):
    left = one_hot(to, to_total, factor)
    right = one_hot(start, start_total)
    batch = tuple(range(to.ndim - 1))
    last = to.ndim
    return lax.dot_general(
        left, right, (((last,), (last,)), (batch, batch)), preferred_element_type=jnp.float32
    ).astype(jnp.bfloat16)


def push_blocks(partials, rows, beside):
    pieces = []
    for column in range(2 * REACH + 1):
        piece = partials[column * rows : (column + 1) * rows]
        offset = column - REACH
        if offset != 0:
            piece = passed_along(piece, ("mesh", "sub"), offset)
        pieces.append(piece)
    pieces, beside = lax.optimization_barrier((pieces, beside))
    summed = pieces[0].astype(jnp.float32)
    for piece in pieces[1:]:
        summed = summed + piece.astype(jnp.float32)
    return summed, beside


def pull_blocks(values):
    pieces = []
    for column in range(2 * REACH + 1):
        offset = column - REACH
        if offset == 0:
            pieces.append(values)
        else:
            pieces.append(passed_along(values, ("mesh", "sub"), -offset))
    return jnp.concatenate(pieces, axis=0)


def send_far(values):
    return lax.all_to_all(values, ("mesh", "sub"), split_axis=0, concat_axis=0, tiled=True)


def added_up(part, axes):
    shards = lax.axis_size(axes)
    count, width = part.shape
    share = -(-count // (16 * shards)) * 16
    part = jnp.pad(part, ((0, share * shards - count), (0, 0))).astype(jnp.bfloat16)
    shares = send_far(part.reshape(shards, share, width))
    total = jnp.sum(shares.astype(jnp.float32), axis=0).astype(jnp.bfloat16)
    spread = send_far(jnp.broadcast_to(total, (shards, share, width)))
    return spread.reshape(-1, width)[:count].astype(jnp.float32)


def contract_rows(left, right):
    return lax.dot_general(
        left, right, (((0,), (0,)), ((), ())), preferred_element_type=jnp.float32
    )


def times(left, right):
    return jnp.dot(left, right, preferred_element_type=jnp.float32)


def times_transpose(left, right):
    return lax.dot_general(
        left, right, (((1,), (1,)), ((), ())), preferred_element_type=jnp.float32
    )


def per_device(
    inputs,
    targets,
    node_weight,
    w_embed,
    w_mix,
    w_back,
    head_projection_weight,
    enc_src,
    enc_dst,
    enc_weight,
    enc_count,
    proc_src,
    proc_dst,
    proc_weight,
    proc_count,
    far_src,
    far_dst,
    far_weight,
    far_count,
    dec_src,
    dec_dst,
    dec_weight,
    dec_count,
):
    shards = lax.axis_size(("mesh", "sub"))
    grid_rows = inputs.shape[0]
    mesh_rows = M_DEV
    total_grid = grid_rows * shards
    pre_embed = jnp.dot(inputs, w_embed, preferred_element_type=jnp.float32)
    embedded = jax.nn.silu(pre_embed).astype(jnp.bfloat16)
    axes = ("mesh", "sub")
    enc_factor = slot_factor(enc_weight[0], enc_count[0])
    enc_matrix = edge_matrix(enc_factor, enc_dst[0], mesh_rows, enc_src[0], grid_rows)
    enc_matrix = enc_matrix.reshape(-1, grid_rows)
    dec_factor = slot_factor(dec_weight[0], dec_count[0])
    dec_matrix = edge_matrix(dec_factor, dec_src[0], mesh_rows, dec_dst[0], grid_rows)
    dec_matrix = dec_matrix.reshape(-1, grid_rows)
    first_node = lax.axis_index(axes) * mesh_rows
    local_src = jnp.mod(proc_src[0] - first_node + HALO, mesh_rows * shards)
    proc_factor = slot_factor(proc_weight, proc_count)[0]
    proc_matrix = edge_matrix(proc_factor, proc_dst[0], mesh_rows, local_src, mesh_rows + 2 * HALO)
    far_factor = slot_factor(far_weight, far_count).reshape(-1)
    far_into = one_hot(far_dst.reshape(-1), mesh_rows, far_factor)
    far_from = one_hot(far_src.reshape(-1), mesh_rows)
    enc_partial = times(enc_matrix, embedded).astype(jnp.bfloat16)
    gathered, (dec_matrix, proc_matrix, far_into, far_from) = push_blocks(
        enc_partial, mesh_rows, (dec_matrix, proc_matrix, far_into, far_from)
    )
    far_shape = far_src.shape + (w_mix.shape[0],)
    mesh_scale = norm_scale(gathered)
    latent_f = gathered * mesh_scale
    mesh_latent = latent_f.astype(jnp.bfloat16)
    far_out = contract_rows(far_from, mesh_latent).astype(jnp.bfloat16)
    far_rows = send_far(far_out.reshape(far_shape)).reshape(-1, far_shape[-1])
    before = passed_along(mesh_latent[mesh_rows - HALO :], axes, 1)
    after = passed_along(mesh_latent[:HALO], axes, -1)
    extended = jnp.concatenate([before, mesh_latent, after], axis=0)
    proc_sum = times(proc_matrix, extended) + times(far_into, far_rows)
    mixed_in = mesh_latent.astype(jnp.float32) + proc_sum
    proc_scale = norm_scale(mixed_in)
    proc_norm = mixed_in * proc_scale
    normed = proc_norm.astype(jnp.bfloat16)
    pre_mix = jnp.dot(normed, w_mix, preferred_element_type=jnp.float32)
    hidden = jax.nn.silu(pre_mix).astype(jnp.bfloat16)
    processed = (
        mesh_latent.astype(jnp.float32)
        + jnp.dot(hidden, w_back, preferred_element_type=jnp.float32)
    ).astype(jnp.bfloat16)
    near_processed = pull_blocks(processed)
    decoded = contract_rows(dec_matrix, near_processed)
    grid_in = embedded.astype(jnp.float32) + decoded
    grid_scale = norm_scale(grid_in)
    grid_norm = grid_in * grid_scale
    grid_node_state = grid_norm.astype(jnp.bfloat16)
    predicted_fields = jnp.dot(
        grid_node_state, head_projection_weight, preferred_element_type=jnp.float32
    )
    residual_error = predicted_fields - targets.astype(jnp.float32)
    loss_part = 0.5 * jnp.sum(node_weight[:, None] * residual_error * residual_error)
    weighted_error = (node_weight[:, None] * residual_error).astype(jnp.bfloat16)
    d_state = times_transpose(weighted_error, head_projection_weight)
    d_grid = norm_back(d_state, grid_norm, grid_scale)
    dec_partial = times(dec_matrix, d_grid.astype(jnp.bfloat16)).astype(jnp.bfloat16)
    head_part = contract_rows(weighted_error, grid_node_state)
    d_processed, (head_part, loss_part) = push_blocks(
        dec_partial, mesh_rows, (head_part, loss_part)
    )
    processed_grad = d_processed.astype(jnp.bfloat16)
    d_pre_mix = (times_transpose(processed_grad, w_back) * silu_slope(pre_mix)).astype(jnp.bfloat16)
    d_normed = times_transpose(d_pre_mix, w_mix)
    d_proc = norm_back(d_normed, proc_norm, proc_scale)
    d_proc_b = d_proc.astype(jnp.bfloat16)
    far_back = send_far(times(far_into.T, d_proc_b).astype(jnp.bfloat16).reshape(far_shape))
    far_spread = times(far_from, far_back.reshape(-1, far_shape[-1]))
    spread = contract_rows(proc_matrix, d_proc_b)
    rims = spread.astype(jnp.bfloat16)
    from_left = passed_along(rims[mesh_rows + HALO :], axes, 1).astype(jnp.float32)
    from_right = passed_along(rims[:HALO], axes, -1).astype(jnp.float32)
    from_left = jnp.pad(from_left, ((0, mesh_rows - HALO), (0, 0)))
    from_right = jnp.pad(from_right, ((mesh_rows - HALO, 0), (0, 0)))
    inner_part = spread[HALO : HALO + mesh_rows]
    width = w_mix.shape[0]
    early_part = jnp.concatenate(
        [
            contract_rows(normed, d_pre_mix),
            contract_rows(hidden, processed_grad),
            head_part,
            jnp.broadcast_to(loss_part, (1, width)),
        ],
        axis=0,
    )
    early_total = lax.psum(early_part, axes)
    d_latent = d_processed + d_proc + inner_part + from_left + from_right + far_spread
    d_gathered = norm_back(d_latent, latent_f, mesh_scale)
    enc_back = d_gathered.astype(jnp.bfloat16)
    near_back = pull_blocks(enc_back)
    d_embedded = d_grid + contract_rows(enc_matrix, near_back)
    d_pre_embed = (d_embedded * silu_slope(pre_embed)).astype(jnp.bfloat16)
    input_gradient = times_transpose(d_pre_embed, w_embed).astype(jnp.bfloat16)
    embed_total = added_up(contract_rows(inputs, d_pre_embed), axes)
    return (
        predicted_fields.astype(jnp.bfloat16),
        input_gradient,
        embed_total / total_grid,
        early_total[:width] / total_grid,
        early_total[width : 2 * width] / total_grid,
        early_total[2 * width : -1].T / total_grid,
        early_total[-1, :1] / total_grid,
    )


def solution(mesh):
    placed = (
        P(("groups", "mesh", "sub"), None),
        P(("groups", "mesh", "sub"), None),
        P(("mesh", "sub")),
        P(),
        P(),
        P(),
        P(),
        P(("mesh", "sub"), None, None),
        P(("mesh", "sub"), None, None),
        P(("mesh", "sub"), None, None),
        P(("mesh", "sub"), None),
        P(("mesh", "sub"), None),
        P(("mesh", "sub"), None),
        P(("mesh", "sub"), None),
        P(("mesh", "sub")),
        P(("mesh", "sub"), None),
        P(("mesh", "sub"), None),
        P(("mesh", "sub"), None),
        P(("mesh", "sub")),
        P(("mesh", "sub"), None, None),
        P(("mesh", "sub"), None, None),
        P(("mesh", "sub"), None, None),
        P(("mesh", "sub"), None),
    )
    return jax.shard_map(
        per_device,
        mesh=mesh,
        in_specs=placed,
        out_specs=(
            P(("groups", "mesh", "sub"), None),
            P(("groups", "mesh", "sub"), None),
            P("groups", None),
            P("groups", None),
            P("groups", None),
            P("groups", None),
            P("groups"),
        ),
        check_vma=False,
    )
```

```python
import jax
import jax.numpy as jnp
from jax import lax
from jax.sharding import PartitionSpec as P

M_DEV = 320
REACH = 2
HALO = 32


EPS = 1e-05


def passed_along(block, axis, distance):
    devices = range(lax.axis_size(axis))
    route = [((i - distance) % len(devices), i) for i in devices]
    return lax.ppermute(block, axis, route)


def norm_scale(values):
    return lax.rsqrt(jnp.mean(values * values, axis=-1, keepdims=True) + EPS)


def norm_back(upstream, normed_f, scale):
    return scale * (upstream - normed_f * jnp.mean(upstream * normed_f, axis=-1, keepdims=True))


def silu_slope(values):
    sigma = jax.nn.sigmoid(values)
    return sigma * (1.0 + values * (1.0 - sigma))


def slot_factor(weight, count):
    live_slot = lax.broadcasted_iota(jnp.int32, weight.shape, 1) < count[:, None]
    return jnp.where(live_slot, weight, 0.0)


def one_hot(index, total, factor=None):
    rows = lax.broadcasted_iota(jnp.int32, index.shape[:-1] + (total, index.shape[-1]), index.ndim - 1)
    hit = rows == index[..., None, :]
    marks = 1.0 if factor is None else factor[..., None, :]
    return jnp.where(hit, marks, 0.0).astype(jnp.bfloat16)


def edge_matrix(factor, to, to_total, start, start_total):
    left = one_hot(to, to_total, factor)
    right = one_hot(start, start_total)
    batch = tuple(range(to.ndim - 1))
    last = to.ndim
    return lax.dot_general(
        left, right, (((last,), (last,)), (batch, batch)), preferred_element_type=jnp.float32
    ).astype(jnp.bfloat16)


def push_blocks(partials, rows, beside):
    pieces = []
    for column in range(2 * REACH + 1):
        piece = partials[column * rows : (column + 1) * rows]
        offset = column - REACH
        if offset != 0:
            piece = passed_along(piece, ("mesh", "sub"), offset)
        pieces.append(piece)
    pieces, beside = lax.optimization_barrier((pieces, beside))
    summed = pieces[0].astype(jnp.float32)
    for piece in pieces[1:]:
        summed = summed + piece.astype(jnp.float32)
    return summed, beside


def pull_blocks(values):
    pieces = []
    for column in range(2 * REACH + 1):
        offset = column - REACH
        if offset == 0:
            pieces.append(values)
        else:
            pieces.append(passed_along(values, ("mesh", "sub"), -offset))
    return jnp.concatenate(pieces, axis=0)


def send_far(values):
    return lax.all_to_all(values, ("mesh", "sub"), split_axis=0, concat_axis=0, tiled=True)


def send_shares(part, axes):
    shards = lax.axis_size(axes)
    count, width = part.shape
    share = -(-count // (16 * shards)) * 16
    part = jnp.pad(part, ((0, share * shards - count), (0, 0))).astype(jnp.bfloat16)
    return send_far(part.reshape(shards, share, width))


def added_up(shares, count):
    width = shares.shape[-1]
    total = jnp.sum(shares.astype(jnp.float32), axis=0).astype(jnp.bfloat16)
    spread = send_far(jnp.broadcast_to(total, shares.shape))
    return spread.reshape(-1, width)[:count].astype(jnp.float32)


def in_pieces(value, width):
    high = lax.reduce_precision(value, 8, 7)
    middle = lax.reduce_precision(value - high, 8, 7)
    pieces = jnp.stack([high, middle, value - high - middle]).reshape(1, 3)
    return jnp.pad(pieces, ((0, 0), (0, width - 3))).astype(jnp.bfloat16)


def contract_rows(left, right):
    return lax.dot_general(
        left, right, (((0,), (0,)), ((), ())), preferred_element_type=jnp.float32
    )


def times(left, right):
    return jnp.dot(left, right, preferred_element_type=jnp.float32)


def times_transpose(left, right):
    return lax.dot_general(
        left, right, (((1,), (1,)), ((), ())), preferred_element_type=jnp.float32
    )


def per_device(
    inputs,
    targets,
    node_weight,
    w_embed,
    w_mix,
    w_back,
    head_projection_weight,
    enc_src,
    enc_dst,
    enc_weight,
    enc_count,
    proc_src,
    proc_dst,
    proc_weight,
    proc_count,
    far_src,
    far_dst,
    far_weight,
    far_count,
    dec_src,
    dec_dst,
    dec_weight,
    dec_count,
):
    shards = lax.axis_size(("mesh", "sub"))
    grid_rows = inputs.shape[0]
    mesh_rows = M_DEV
    total_grid = grid_rows * shards
    pre_embed = jnp.dot(inputs, w_embed, preferred_element_type=jnp.float32)
    embedded = jax.nn.silu(pre_embed).astype(jnp.bfloat16)
    axes = ("mesh", "sub")
    enc_factor = slot_factor(enc_weight[0], enc_count[0])
    enc_matrix = edge_matrix(enc_factor, enc_dst[0], mesh_rows, enc_src[0], grid_rows)
    enc_matrix = enc_matrix.reshape(-1, grid_rows)
    dec_factor = slot_factor(dec_weight[0], dec_count[0])
    dec_matrix = edge_matrix(dec_factor, dec_src[0], mesh_rows, dec_dst[0], grid_rows)
    dec_matrix = dec_matrix.reshape(-1, grid_rows)
    first_node = lax.axis_index(axes) * mesh_rows
    local_src = jnp.mod(proc_src[0] - first_node + HALO, mesh_rows * shards)
    proc_factor = slot_factor(proc_weight, proc_count)[0]
    proc_matrix = edge_matrix(proc_factor, proc_dst[0], mesh_rows, local_src, mesh_rows + 2 * HALO)
    far_factor = slot_factor(far_weight, far_count).reshape(-1)
    far_into = one_hot(far_dst.reshape(-1), mesh_rows, far_factor)
    far_from = one_hot(far_src.reshape(-1), mesh_rows)
    enc_partial = times(enc_matrix, embedded).astype(jnp.bfloat16)
    gathered, (dec_matrix, proc_matrix, far_into, far_from) = push_blocks(
        enc_partial, mesh_rows, (dec_matrix, proc_matrix, far_into, far_from)
    )
    far_shape = far_src.shape + (w_mix.shape[0],)
    mesh_scale = norm_scale(gathered)
    latent_f = gathered * mesh_scale
    mesh_latent = latent_f.astype(jnp.bfloat16)
    far_out = contract_rows(far_from, mesh_latent).astype(jnp.bfloat16)
    far_rows = send_far(far_out.reshape(far_shape)).reshape(-1, far_shape[-1])
    before = passed_along(mesh_latent[mesh_rows - HALO :], axes, 1)
    after = passed_along(mesh_latent[:HALO], axes, -1)
    extended = jnp.concatenate([before, mesh_latent, after], axis=0)
    proc_sum = times(proc_matrix, extended) + times(far_into, far_rows)
    mixed_in = mesh_latent.astype(jnp.float32) + proc_sum
    proc_scale = norm_scale(mixed_in)
    proc_norm = mixed_in * proc_scale
    normed = proc_norm.astype(jnp.bfloat16)
    pre_mix = jnp.dot(normed, w_mix, preferred_element_type=jnp.float32)
    hidden = jax.nn.silu(pre_mix).astype(jnp.bfloat16)
    processed = (
        mesh_latent.astype(jnp.float32)
        + jnp.dot(hidden, w_back, preferred_element_type=jnp.float32)
    ).astype(jnp.bfloat16)
    near_processed = pull_blocks(processed)
    decoded = contract_rows(dec_matrix, near_processed)
    grid_in = embedded.astype(jnp.float32) + decoded
    grid_scale = norm_scale(grid_in)
    grid_norm = grid_in * grid_scale
    grid_node_state = grid_norm.astype(jnp.bfloat16)
    predicted_fields = jnp.dot(
        grid_node_state, head_projection_weight, preferred_element_type=jnp.float32
    )
    residual_error = predicted_fields - targets.astype(jnp.float32)
    loss_part = 0.5 * jnp.sum(node_weight[:, None] * residual_error * residual_error)
    weighted_error = (node_weight[:, None] * residual_error).astype(jnp.bfloat16)
    d_state = times_transpose(weighted_error, head_projection_weight)
    d_grid = norm_back(d_state, grid_norm, grid_scale)
    dec_partial = times(dec_matrix, d_grid.astype(jnp.bfloat16)).astype(jnp.bfloat16)
    head_part = contract_rows(weighted_error, grid_node_state)
    d_processed, (head_part, loss_part) = push_blocks(
        dec_partial, mesh_rows, (head_part, loss_part)
    )
    processed_grad = d_processed.astype(jnp.bfloat16)
    d_pre_mix = (times_transpose(processed_grad, w_back) * silu_slope(pre_mix)).astype(jnp.bfloat16)
    d_normed = times_transpose(d_pre_mix, w_mix)
    d_proc = norm_back(d_normed, proc_norm, proc_scale)
    d_proc_b = d_proc.astype(jnp.bfloat16)
    far_term = times(far_into.T, d_proc_b).astype(jnp.bfloat16).reshape(far_shape)
    loss_row = jnp.broadcast_to(in_pieces(loss_part, far_shape[-1]), (shards, 1, far_shape[-1]))
    far_back = send_far(jnp.concatenate([far_term, loss_row], axis=1))
    loss_total = jnp.sum(far_back[:, -1].astype(jnp.float32)).reshape(1)
    far_spread = times(far_from, far_back[:, :-1].reshape(-1, far_shape[-1]))
    spread = contract_rows(proc_matrix, d_proc_b)
    rims = spread.astype(jnp.bfloat16)
    from_left = passed_along(rims[mesh_rows + HALO :], axes, 1).astype(jnp.float32)
    from_right = passed_along(rims[:HALO], axes, -1).astype(jnp.float32)
    from_left = jnp.pad(from_left, ((0, mesh_rows - HALO), (0, 0)))
    from_right = jnp.pad(from_right, ((mesh_rows - HALO, 0), (0, 0)))
    inner_part = spread[HALO : HALO + mesh_rows]
    width = w_mix.shape[0]
    d_latent = d_processed + d_proc + inner_part + from_left + from_right + far_spread
    d_gathered = norm_back(d_latent, latent_f, mesh_scale)
    enc_back = d_gathered.astype(jnp.bfloat16)
    near_back = pull_blocks(enc_back)
    d_embedded = d_grid + contract_rows(enc_matrix, near_back)
    d_pre_embed = (d_embedded * silu_slope(pre_embed)).astype(jnp.bfloat16)
    input_gradient = times_transpose(d_pre_embed, w_embed).astype(jnp.bfloat16)
    gradients = jnp.concatenate(
        [
            contract_rows(normed, d_pre_mix).astype(jnp.bfloat16),
            contract_rows(hidden, processed_grad).astype(jnp.bfloat16),
            head_part.astype(jnp.bfloat16),
            contract_rows(inputs, d_pre_embed).astype(jnp.bfloat16),
        ],
        axis=0,
    )
    totals = added_up(send_shares(gradients, axes), gradients.shape[0]) / total_grid
    head_end = 2 * width + head_part.shape[0]
    return (
        predicted_fields.astype(jnp.bfloat16),
        input_gradient,
        totals[head_end:],
        totals[:width],
        totals[width : 2 * width],
        totals[2 * width : head_end].T,
        loss_total / total_grid,
    )


def solution(mesh):
    placed = (
        P(("groups", "mesh", "sub"), None),
        P(("groups", "mesh", "sub"), None),
        P(("mesh", "sub")),
        P(),
        P(),
        P(),
        P(),
        P(("mesh", "sub"), None, None),
        P(("mesh", "sub"), None, None),
        P(("mesh", "sub"), None, None),
        P(("mesh", "sub"), None),
        P(("mesh", "sub"), None),
        P(("mesh", "sub"), None),
        P(("mesh", "sub"), None),
        P(("mesh", "sub")),
        P(("mesh", "sub"), None),
        P(("mesh", "sub"), None),
        P(("mesh", "sub"), None),
        P(("mesh", "sub")),
        P(("mesh", "sub"), None, None),
        P(("mesh", "sub"), None, None),
        P(("mesh", "sub"), None, None),
        P(("mesh", "sub"), None),
    )
    return jax.shard_map(
        per_device,
        mesh=mesh,
        in_specs=placed,
        out_specs=(
            P(("groups", "mesh", "sub"), None),
            P(("groups", "mesh", "sub"), None),
            P("groups", None),
            P("groups", None),
            P("groups", None),
            P("groups", None),
            P("groups"),
        ),
        check_vma=False,
    )
```
